128 devices in a mesh: energy: 4 (over x_lo, core), row: 8 (over x_hi, y), col: 4 (over z).
Axes of the slice: x: 4 (x_hi: 2, x_lo: 2; x = x_hi * 2 + x_lo), y: 4, z: 4, core: 2. Of those that a mesh axis runs over, the one named last changes fastest.
Arguments:
- green: bfloat16 [4, 2, 8192, 2048], P('energy', None, 'row', 'col'), may hold values from -0.890625 to 0.890625
- broadening: bfloat16 [4, 2, 2048, 2048], P('energy', None, None, 'col'), may hold values from -34 to 34, as said below
- quad_weight: float32 [4], P('energy'), may hold values from 0.25 to 1
- pair_cols: int32 [2048], P('row'), may hold values from 0 to 127, as said below
Outputs:
- density: float32 [8, 256, 64, 128], P('row', ('energy', 'col'))
The draws below stay inside these ranges and needn't reach their ends.
Inputs may be any that keep to these rules, and one draw needn't show every extreme that they name: broadening[e] is exactly Hermitian (real part symmetric, imaginary part antisymmetric). `pair_cols`: pattern block q lies in slab s = q // 256, and its block column lies in slabs s - 1, s or s + 1 (block columns of slab t are t * 16 to (t + 1) * 16 - 1).
All inputs are finite; a program needn't handle non-finite values.
Results may differ from the reference program's by a relative error of at most 0.0018.
Values may be sent and summed in bfloat16 or wider, within the bound.
A program may use at most 128 MiB of HBM per device.

```python
import math
import jax
import jax.numpy as jnp
from jax import lax

BLOCK = 64
M = 2048
BLK_DEV = 16
PB = 16
PAIRS_DEV = 256
ENERGIES = 4
NSLAB = 8
NORB = 8192
NBLK = 128
PAIRS = 2048


def draw_broadening(key, part):
    key = jax.random.fold_in(key, 11)
    key_re, key_im, key_diag = jax.random.split(key, 3)
    offdiag = 0.5 * M ** (-0.5)
    raw_re = offdiag * jnp.clip(jax.random.normal(key_re, (ENERGIES, M, M), jnp.float32), -6.0, 6.0)
    raw_im = offdiag * jnp.clip(jax.random.normal(key_im, (ENERGIES, M, M), jnp.float32), -6.0, 6.0)
    diag_vals = jax.random.uniform(key_diag, (ENERGIES, M), jnp.float32, 1.0, 2.0)
    eye_mask = jnp.eye(M, dtype=jnp.float32)
    sym_re = raw_re + jnp.swapaxes(raw_re, 1, 2)
    sym_re = sym_re * (1.0 - eye_mask) + eye_mask * diag_vals[:, :, None]
    anti_im = raw_im - jnp.swapaxes(raw_im, 1, 2)
    return jnp.stack([sym_re, anti_im], axis=1).astype(jnp.bfloat16)


def draw_pair_cols(key, part):
    key = jax.random.fold_in(key, 23)
    index = jnp.arange(PAIRS, dtype=jnp.int32)
    slab = index // PAIRS_DEV
    low = jnp.maximum(slab - 1, 0) * BLK_DEV
    high = jnp.minimum(slab + 2, NSLAB) * BLK_DEV
    cols = jax.random.randint(key, (PAIRS,), low, high, jnp.int32)
    cols = cols.at[0].set(0)
    cols = cols.at[PAIRS - 1].set(NBLK - 1)
    return cols


def steps_of(key, shape, cuts, least, largest):
    def one(dim, shards_of):
        heights = jax.random.uniform(jax.random.fold_in(jax.random.fold_in(key, 6), dim), (shards_of,), jnp.float32, least / len(cuts), largest / len(cuts))
        return jnp.repeat(jnp.exp(heights), shape[dim] // shards_of).reshape((-1,) + (1,) * (len(shape) - dim - 1))

    loudness = one(*cuts[0])
    for cut in cuts[1:]:
        loudness = loudness * one(*cut)
    return loudness


def normal_values(key, dims, width, reach, cuts=(), kind=jnp.bfloat16):
    entries = jax.random.normal(key, dims, jnp.float32) * width
    if len(cuts) > 0:
        entries = steps_of(key, dims, cuts, -0.22, 0.18) * entries
    return jnp.clip(entries, min=-reach, max=reach).astype(kind)


def setup_inputs(seed: int = 0) -> dict:
    seeds = jax.random.split(jax.random.key(seed), 5)
    green = normal_values(seeds[0], (ENERGIES, 2, NORB, M), (M ** -0.25), 0.890625, ((0, 4), (2, 8), (3, 4)))
    broadening = draw_broadening(jax.random.fold_in(seeds[4], 71), 0)
    quad_weight = jnp.clip(jnp.exp(math.log(1.0) - 1.3862944 * jax.random.uniform(seeds[2], (ENERGIES,), jnp.float32) ** steps_of(seeds[2], (ENERGIES,), ((0, 4),), -0.2, 0.2)), 0.25, 1.0)
    pair_cols = draw_pair_cols(jax.random.fold_in(seeds[4], 71), 0)
    return {"green": green, "broadening": broadening, "quad_weight": quad_weight, "pair_cols": pair_cols}


def complex_dot(left_re, left_im, right_re, right_im):
    real_part = jnp.dot(left_re, right_re, preferred_element_type=jnp.float32) - jnp.dot(left_im, right_im, preferred_element_type=jnp.float32)
    imag_part = jnp.dot(left_re, right_im, preferred_element_type=jnp.float32) + jnp.dot(left_im, right_re, preferred_element_type=jnp.float32)
    return real_part, imag_part


def reference(green, broadening, quad_weight, pair_cols):
    total = jnp.zeros((NSLAB, PAIRS_DEV, BLOCK, 2 * BLOCK), jnp.float32)
    for energy_idx in range(ENERGIES):
        spec_re, spec_im = complex_dot(green[energy_idx, 0], green[energy_idx, 1], broadening[energy_idx, 0], broadening[energy_idx, 1])
        spec_re = spec_re.astype(jnp.bfloat16).reshape(NBLK, BLOCK, M)
        spec_im = spec_im.astype(jnp.bfloat16).reshape(NBLK, BLOCK, M)
        green_re = green[energy_idx, 0].reshape(NBLK, BLOCK, M)
        green_im = green[energy_idx, 1].reshape(NBLK, BLOCK, M)

        def one_slab(slab):
            start = (slab * BLK_DEV).astype(jnp.int32)
            wre = lax.dynamic_slice_in_dim(spec_re, start, BLK_DEV, 0).astype(jnp.float32)
            wim = lax.dynamic_slice_in_dim(spec_im, start, BLK_DEV, 0).astype(jnp.float32)
            cols = lax.dynamic_slice_in_dim(pair_cols, (slab * PAIRS_DEV).astype(jnp.int32), PAIRS_DEV, 0).reshape(BLK_DEV, PB)
            gre = jnp.take(green_re, cols, axis=0).astype(jnp.float32)
            gim = jnp.take(green_im, cols, axis=0).astype(jnp.float32)
            real_part = jnp.einsum("bam,bkcm->bkac", wre, gre) + jnp.einsum("bam,bkcm->bkac", wim, gim)
            imag_part = jnp.einsum("bam,bkcm->bkac", wim, gre) - jnp.einsum("bam,bkcm->bkac", wre, gim)
            joined = jnp.concatenate([real_part, imag_part], axis=-1)
            return joined.reshape(PAIRS_DEV, BLOCK, 2 * BLOCK)

        slabs = lax.map(one_slab, jnp.arange(NSLAB, dtype=jnp.int32))
        total = total + quad_weight[energy_idx] * slabs
    return total
```

```python
import functools

import jax
import jax.numpy as jnp
from jax import lax
from jax.experimental import pallas as pl
from jax.experimental.pallas import tpu as pltpu
from jax.sharding import PartitionSpec as P

MESH = pl.DeviceIdType.MESH
NT = (((1,), (1,)), ((), ()))
BLOCK = 64
PB = 16
TOP = 32766.0
CHUNKS = 8
LEAD = 2


def encode(total, codes, scale):
    peak = jnp.maximum(jnp.max(jnp.abs(total), axis=0, keepdims=True), 1e-30)
    codes[...] = jnp.round(total * (TOP / peak)).astype(jnp.int32).astype(jnp.int16)
    scale[...] = jnp.broadcast_to(peak * (1.0 / TOP), scale.shape)


def decode(codes, scale):
    return codes[...].astype(jnp.int32).astype(jnp.float32) * scale[0:1, :]


def kernel(
    green, gamma, weight, pairs, out,
    gall, near, gam, spec, csend, crecv, xsend, xrecv, xsscale, xrscale, zsend, zrecv, zsscale, zrscale, own,
    loc, gs, gr, rs, rr, ys, yr, cs, cr, xs, xr, xss, xrs, zs, zr, zss, zrs,
):
    e, r, c = lax.axis_index("energy"), lax.axis_index("row"), lax.axis_index("col")
    xbit, core = e // 2, e % 2
    up, down, over = (c + 1) % 4, (c + 3) % 4, (c + 2) % 4
    above, below = (r + 1) % 8, (r + 7) % 8
    core_peer, x_peer = (e + 1 - 2 * core, r, c), (e + 2 - 4 * xbit, r, c)
    z_up, z_down = (e, r, up), (e, r, down)

    def cols(owner):
        return pl.ds(pl.multiple_of(owner * 512, 512), 512)

    def block_of(u, half):
        dx, kp, dk = 1 - u // 4, (u // 2) % 2, 1 - u % 2
        return ((xbit + dx) % 2) * 8 + ((core + dk) % 2) * 4 + kp * 2 + half

    def rows_of(u, half=0, count=2):
        return pl.ds(block_of(u, half), count)

    def remote(src, dst, send, recv, peer):
        return pltpu.make_async_remote_copy(
            src_ref=src, dst_ref=dst, send_sem=send, recv_sem=recv, device_id=peer, device_id_type=MESH
        )

    def hand(u, way):
        return remote(
            green.at[0, :, rows_of(u)], gall.at[:, rows_of(u), :, cols(c)],
            gs.at[way, u], gr.at[way, u], (z_up, z_down)[way],
        )

    def handed(u, way):
        origin = (down, up)[way]
        return remote(
            green.at[0, :, rows_of(u)], gall.at[:, rows_of(u), :, cols(origin)],
            gs.at[way, u], gr.at[way, u], (z_up, z_down)[way],
        )

    def relay(u, way):
        piece = gall.at[:, rows_of(u, way, 1), :, cols((down, up)[way])]
        return remote(piece, piece, rs.at[way, u], rr.at[way, u], (z_up, z_down)[way])

    def relayed(u, way):
        piece = gall.at[:, rows_of(u, way, 1), :, cols(over)]
        return remote(piece, piece, rs.at[way, u], rr.at[way, u], (z_up, z_down)[way])

    def halo(way):
        return remote(
            green.at[0], near.at[:, pl.ds(32 * way, 16)], ys.at[way], yr.at[way],
            (e, (above, below)[way], c),
        )

    def core_copy(n):
        return remote(csend.at[n], crecv.at[n], cs.at[n], cr.at[n], core_peer)

    def x_copies(n):
        return (
            remote(xsend.at[n], xrecv.at[n], xs.at[n], xr.at[n], x_peer),
            remote(xsscale.at[n], xrscale.at[n], xss.at[n], xrs.at[n], x_peer),
        )

    def z_copies(k, slot):
        return (
            remote(zsend.at[k], zrecv.at[slot], zs.at[k], zr.at[slot], (e, r, k)),
            remote(zsscale.at[k], zrscale.at[slot], zss.at[k], zrs.at[slot], (e, r, k)),
        )

    locals_ = [
        pltpu.make_async_copy(green.at[0], gall.at[:, :, :, cols(c)], loc.at[0]),
        pltpu.make_async_copy(gamma.at[0], gam, loc.at[1]),
        pltpu.make_async_copy(green.at[0], near.at[:, pl.ds(16, 16)], loc.at[2]),
    ]
    for copy in locals_:
        copy.start()

    barrier = pltpu.get_barrier_semaphore()
    peers = (core_peer, x_peer, z_up, z_down, (e, r, over), (e, above, c), (e, below, c))
    for peer in peers:
        pl.semaphore_signal(barrier, inc=1, device_id=peer, device_id_type=MESH)
    pl.semaphore_wait(barrier, len(peers))

    for u in range(LEAD):
        for way in range(2):
            hand(u, way).start()
    for way in range(2):
        halo(way).start()
    for copy in locals_:
        copy.wait()

    def feed(t):
        @pl.when(t < CHUNKS - LEAD)
        def _():
            for way in range(2):
                hand(t + LEAD, way).start()

        @pl.when(t < CHUNKS)
        def _():
            for way in range(2):
                handed(t, way).wait_recv()
                relay(t, way).start()

    def spectral(u):
        for way in range(2):
            relayed(u, way).wait_recv()
        first = block_of(u, 0)
        left = gall[:, rows_of(u)].reshape(256, 2048)
        with_re = jnp.dot(left, gam[0], preferred_element_type=jnp.float32)
        with_im = jnp.dot(left, gam[1], preferred_element_type=jnp.float32)
        re = (with_re[:128] - with_im[128:]).astype(jnp.bfloat16)
        im = (with_im[:128] + with_re[128:]).astype(jnp.bfloat16)
        for half in range(2):
            a, b = re[half * BLOCK : (half + 1) * BLOCK], im[half * BLOCK : (half + 1) * BLOCK]
            spec[first + half, 0:BLOCK, 0:512] = a
            spec[first + half, 0:BLOCK, 512:1024] = b
            spec[first + half, BLOCK:128, 0:512] = b
            spec[first + half, BLOCK:128, 512:1024] = -a

    def terms(u, half):
        block = block_of(u, half)
        at = [jnp.clip(pairs[block * PB + p] - (r - 1) * PB, 0, 47) for p in range(PB)]
        right_re = jnp.concatenate([near[0, o] for o in at], axis=0)
        right_im = jnp.concatenate([near[1, o] for o in at], axis=0)
        left = spec[block]
        found = lax.dot_general(right_re, left[:, :512], NT, preferred_element_type=jnp.float32)
        found += lax.dot_general(right_im, left[:, 512:], NT, preferred_element_type=jnp.float32)
        return found * weight[0]

    def step(t, carry):
        feed(t)

        @pl.when(t > 0)
        def _():
            spectral(t - 1)

        return carry

    lax.fori_loop(0, 5, step, 0)
    for way in range(2):
        halo(way).wait_recv()

    def late_step(g, carry):
        feed(g + 5)
        spectral(g + 4)

        def give(half, inner):
            n = g * 2 + half
            csend[n] = terms(2 * g, half)
            core_copy(n).start()
            return inner

        lax.fori_loop(0, 2, give, 0)

        def keep(half, inner):
            n = g * 2 + half
            mine = terms(2 * g + 1, half)
            core_copy(n).wait_recv()
            total = mine + crecv[n]

            @pl.when(g < 2)
            def _():
                encode(total, xsend.at[n], xsscale.at[n])
                for copy in x_copies(n):
                    copy.start()

            @pl.when(g >= 2)
            def _():
                k = n - 4
                for copy in x_copies(k):
                    copy.wait_recv()
                both = total + decode(xrecv[k], xrscale[k])

                @pl.when(k == c)
                def _():
                    own[...] = both

                @pl.when(k != c)
                def _():
                    encode(both, zsend.at[k], zsscale.at[k])
                    for copy in z_copies(k, (c - k + 3) % 4):
                        copy.start()

            return inner

        lax.fori_loop(0, 2, keep, 0)
        return carry

    lax.fori_loop(0, 4, late_step, 0)

    total = own[...]
    for slot in range(3):
        for copy in z_copies((c + 1) % 4, slot):
            copy.wait_recv()
        total = total + decode(zrecv[slot], zrscale[slot])
    own[...] = total
    for p in range(PB):
        turned = own[p * BLOCK : (p + 1) * BLOCK, :].T
        out[0, p, :, 0:BLOCK] = turned[0:BLOCK]
        out[0, p, :, BLOCK:128] = turned[BLOCK:128]

    def sent(u, carry):
        for way in range(2):
            hand(u, way).wait_send()
            relay(u, way).wait_send()
        core_copy(u).wait_send()
        return carry

    lax.fori_loop(0, CHUNKS, sent, 0)
    for way in range(2):
        halo(way).wait_send()
    for n in range(4):
        for copy in x_copies(n):
            copy.wait_send()
    for step_ in range(1, 4):
        for copy in z_copies((c + step_) % 4, 0):
            copy.wait_send()


def body(green, broadening, quad_weight, pair_cols):
    vmem, smem = pl.BlockSpec(memory_space=pltpu.VMEM), pl.BlockSpec(memory_space=pltpu.SMEM)
    hbm = pl.BlockSpec(memory_space=pl.ANY)
    dma = pltpu.SemaphoreType.DMA
    return pl.pallas_call(
        kernel,
        out_shape=jax.ShapeDtypeStruct((1, PB, BLOCK, 2 * BLOCK), jnp.float32),
        in_specs=[hbm, hbm, smem, smem],
        out_specs=vmem,
        scratch_shapes=[
            pltpu.VMEM((2, 16, BLOCK, 2048), jnp.bfloat16),
            pltpu.VMEM((2, 48, BLOCK, 512), jnp.bfloat16),
            pltpu.VMEM((2, 2048, 512), jnp.bfloat16),
            pltpu.VMEM((16, 128, 1024), jnp.bfloat16),
            pltpu.VMEM((8, 1024, 128), jnp.float32),
            pltpu.VMEM((8, 1024, 128), jnp.float32),
            pltpu.VMEM((4, 1024, 128), jnp.int16),
            pltpu.VMEM((4, 1024, 128), jnp.int16),
            pltpu.VMEM((4, 8, 128), jnp.float32),
            pltpu.VMEM((4, 8, 128), jnp.float32),
            pltpu.VMEM((4, 1024, 128), jnp.int16),
            pltpu.VMEM((3, 1024, 128), jnp.int16),
            pltpu.VMEM((4, 8, 128), jnp.float32),
            pltpu.VMEM((3, 8, 128), jnp.float32),
            pltpu.VMEM((1024, 128), jnp.float32),
            dma((3,)),
            dma((2, CHUNKS)), dma((2, CHUNKS)), dma((2, CHUNKS)), dma((2, CHUNKS)),
            dma((2,)), dma((2,)),
            dma((8,)), dma((8,)),
            dma((4,)), dma((4,)), dma((4,)), dma((4,)),
            dma((4,)), dma((3,)), dma((4,)), dma((3,)),
        ],
        compiler_params=pltpu.CompilerParams(
            collective_id=0, has_side_effects=True, vmem_limit_bytes=56 * 1024 * 1024
        ),
        cost_estimate=pl.CostEstimate(flops=13 * 10**9, bytes_accessed=7 * 2**20, transcendentals=0),
        name="density",
    )(green.reshape(1, 2, 16, BLOCK, 512), broadening, quad_weight, pair_cols)


def solution(mesh):
    placed = (
        P("energy", None, "row", "col"),
        P("energy", None, None, "col"),
        P("energy"),
        P("row"),
    )
    return jax.shard_map(
        body,
        mesh=mesh,
        in_specs=placed,
        out_specs=P("row", ("energy", "col"), None, None),
        check_vma=False,
    )
```

```python
import functools

import jax
import jax.numpy as jnp
from jax import lax
from jax.experimental import pallas as pl
from jax.experimental.pallas import tpu as pltpu
from jax.sharding import PartitionSpec as P

MESH = pl.DeviceIdType.MESH
NT = (((1,), (1,)), ((), ()))
BLOCK = 64
PB = 16
TOP = 32766.0
STEPS = 16
LEAD = 3
EARLY = 11


def scaled(total, peak):
    peak = jnp.maximum(peak, 1e-30)
    return total * (TOP / peak), peak * (1.0 / TOP)


def coded(values):
    return jnp.round(values).astype(jnp.int32).astype(jnp.int16)


def encode(total, codes, scale):
    values, unit = scaled(total, jnp.max(jnp.abs(total), axis=0, keepdims=True))
    codes[...] = coded(values)
    scale[...] = jnp.broadcast_to(unit, scale.shape)


def decode(codes, scale):
    return codes[...].astype(jnp.int32).astype(jnp.float32) * scale[0:1, :]


def kernel(
    green, gamma, weight, pairs, out,
    held, near_a, near_b, begun, mine, theirs, turn, given, spec, psend, precv, psscale, prscale,
    csend, crecv, xsend, xrecv, xsscale, xrscale, zsend, zrecv, zsscale, zrscale, own,
    loc, ws, wr, gs, gr, ps, pr, pss, prs, ys, yr, cs, cr, xs, xr, xss, xrs, zs, zr, zss, zrs,
):
    near = (near_a, near_b)
    e, r, c = lax.axis_index("energy"), lax.axis_index("row"), lax.axis_index("col")
    xbit, core = e // 2, e % 2
    pair, cross = c + 1 - 2 * (c % 2), 3 - c
    above, below = (r + 1) % 8, (r + 7) % 8
    core_peer, x_peer = (e + 1 - 2 * core, r, c), (e + 2 - 4 * xbit, r, c)
    pair_peer, cross_peer = (e, r, pair), (e, r, cross)

    def quarter(owner, count=512):
        return pl.ds(pl.multiple_of(owner * 512, 512), count)

    def block_of(u):
        dx, dk, k = 1 - u // 8, 1 - u % 2, (u % 8) // 2
        return ((xbit + dx) % 2) * 8 + ((core + dk) % 2) * 4 + k

    def remote(src, dst, send, recv, peer):
        return pltpu.make_async_remote_copy(
            src_ref=src, dst_ref=dst, send_sem=send, recv_sem=recv, device_id=peer, device_id_type=MESH
        )

    def hand(u):
        b = block_of(u)
        return remote(
            green.at[0, :, b], held.at[:, b, :, pl.ds(512, 512)], gs.at[u], gr.at[u], cross_peer
        )

    def weights():
        return (
            remote(gamma.at[0, :, quarter(3 - pair, 256), :], given, ws.at[0], wr.at[0], cross_peer),
            remote(
                gamma.at[0, :, quarter(3 - pair), pl.ds(256, 256)],
                theirs.at[:, pl.ds(512, 512), pl.ds(256, 256)], ws.at[1], wr.at[1], pair_peer,
            ),
        )

    def part_copies(u):
        return (
            remote(psend.at[u], precv.at[u], ps.at[u], pr.at[u], pair_peer),
            remote(psscale.at[u], prscale.at[u], pss.at[u], prs.at[u], pair_peer),
        )

    def halo(way, part):
        return remote(
            green.at[0, :, :, :, pl.ds(256 * part, 256)], near[part].at[:, pl.ds(32 * way, 16)],
            ys.at[way, part], yr.at[way, part], (e, (above, below)[way], c),
        )

    def core_copy(n):
        return remote(csend.at[n], crecv.at[n], cs.at[n], cr.at[n], core_peer)

    def x_copies(n):
        return (
            remote(xsend.at[n], xrecv.at[n], xs.at[n], xr.at[n], x_peer),
            remote(xsscale.at[n], xrscale.at[n], xss.at[n], xrs.at[n], x_peer),
        )

    def z_copies(k, slot):
        return (
            remote(zsend.at[k], zrecv.at[slot], zs.at[k], zr.at[slot], (e, r, k)),
            remote(zsscale.at[k], zrscale.at[slot], zss.at[k], zrs.at[slot], (e, r, k)),
        )

    locals_ = [
        pltpu.make_async_copy(gamma.at[0, :, quarter(pair), :], turn, loc.at[0]),
        pltpu.make_async_copy(gamma.at[0, :, quarter(c), :], mine.at[:, pl.ds(0, 512), :], loc.at[1]),
        pltpu.make_async_copy(gamma.at[0, :, quarter(cross), :], mine.at[:, pl.ds(512, 512), :], loc.at[2]),
        pltpu.make_async_copy(green.at[0], held.at[:, :, :, pl.ds(0, 512)], loc.at[3]),
        pltpu.make_async_copy(green.at[0, :, :, :, pl.ds(0, 256)], near_a.at[:, pl.ds(16, 16)], loc.at[4]),
        pltpu.make_async_copy(green.at[0, :, :, :, pl.ds(256, 256)], near_b.at[:, pl.ds(16, 16)], loc.at[5]),
    ]
    for copy in locals_:
        copy.start()

    barrier = pltpu.get_barrier_semaphore()
    peers = (core_peer, x_peer, pair_peer, cross_peer, (e, r, (c + 2) % 4), (e, above, c), (e, below, c))
    for peer in peers:
        pl.semaphore_signal(barrier, inc=1, device_id=peer, device_id_type=MESH)
    pl.semaphore_wait(barrier, len(peers))

    for copy in weights():
        copy.start()
    for u in range(LEAD):
        hand(u).start()
    for way in range(2):
        halo(way, 0).start()
    for copy in locals_:
        copy.wait()
    theirs[0, 0:512, :] = turn[0].T
    theirs[1, 0:512, :] = -(turn[1].T)
    for copy in weights():
        copy.wait_recv()
    theirs[0, 512:1024, 0:256] = given[0].T
    theirs[1, 512:1024, 0:256] = -(given[1].T)

    def product(b, right):
        left = held[:, b].reshape(2 * BLOCK, 1024)
        with_re = jnp.dot(left, right[0], preferred_element_type=jnp.float32)
        with_im = jnp.dot(left, right[1], preferred_element_type=jnp.float32)
        return jnp.concatenate(
            [with_re[:BLOCK] - with_im[BLOCK:], with_im[:BLOCK] + with_re[BLOCK:]], axis=1
        )

    def forward(u):
        @pl.when(u < STEPS - LEAD)
        def _():
            hand(u + LEAD).start()

        hand(u).wait_recv()
        part = product(block_of(u), theirs)
        peak = jnp.max(jnp.abs(part), axis=0, keepdims=True)
        peak = functools.reduce(jnp.maximum, [peak[:, 128 * i : 128 * (i + 1)] for i in range(8)])
        wide = jnp.concatenate([peak] * 8, axis=1)
        values, unit = scaled(part, wide)
        psend[u] = coded(values)
        psscale[u] = jnp.broadcast_to(unit[:, 0:128], (8, 128))
        for copy in part_copies(u):
            copy.start()

    def spectral(u):
        b = block_of(u)
        part = product(b, mine)
        for copy in part_copies(u):
            copy.wait_recv()
        unit = jnp.concatenate([prscale[u][0:1, :]] * 8, axis=1)
        whole = part + precv[u].astype(jnp.int32).astype(jnp.float32) * unit
        whole = whole.astype(jnp.bfloat16)
        spec[b, 0:BLOCK, :] = whole
        spec[b, BLOCK:128, 0:512] = whole[:, 512:]
        spec[b, BLOCK:128, 512:1024] = -whole[:, :512]

    def terms(dx, dk, k, part):
        block = ((xbit + dx) % 2) * 8 + ((core + dk) % 2) * 4 + k
        at = [jnp.clip(pairs[block * PB + p] - (r - 1) * PB, 0, 47) for p in range(PB)]
        right_re = jnp.concatenate([near[part][0, o] for o in at], axis=0)
        right_im = jnp.concatenate([near[part][1, o] for o in at], axis=0)
        left_re = spec[block, :, 256 * part : 256 * part + 256]
        left_im = spec[block, :, 512 + 256 * part : 768 + 256 * part]
        found = lax.dot_general(right_re, left_re, NT, preferred_element_type=jnp.float32)
        return found + lax.dot_general(right_im, left_im, NT, preferred_element_type=jnp.float32)

    def both(dx, dk, k):
        n = 2 * k + 1 - dk
        first = begun[n] if dx else terms(dx, dk, k, 0)
        return (first + terms(dx, dk, k, 1)) * weight[0]

    def give(dx, k):
        n = (1 - dx) * 4 + k
        csend[n] = both(dx, 1, k)
        core_copy(n).start()

    def kept(dx, k):
        n = (1 - dx) * 4 + k
        found = both(dx, 0, k)
        core_copy(n).wait_recv()
        return found + crecv[n]

    def class_of(s):
        return jnp.where(s == 3, c, jnp.where(s < c, s, s + 1))

    def step(u, carry):
        @pl.when(u < STEPS)
        def _():
            forward(u)

        @pl.when(u > 1)
        def _():
            spectral(u - 2)

        return carry

    def step_and_begin(u, carry):
        step(u, carry)
        n = u - 3
        begun[n] = terms(1, 1 - n % 2, n // 2, 0)
        return carry

    lax.fori_loop(0, 2, step, 0)
    for way in range(2):
        halo(way, 1).start()
    lax.fori_loop(2, 3, step, 0)
    for way in range(2):
        halo(way, 0).wait_recv()
    lax.fori_loop(3, EARLY, step_and_begin, 0)
    for way in range(2):
        halo(way, 1).wait_recv()
    give(1, class_of(0))

    def early(s, carry):
        k = class_of(s)

        @pl.when(s < 3)
        def _():
            give(1, class_of(s + 1))

        encode(kept(1, k), xsend.at[k], xsscale.at[k])
        for copy in x_copies(k):
            copy.start()
        return step(EARLY + s, carry)

    lax.fori_loop(0, 4, early, 0)

    def last(s):
        k = class_of(s)
        total = kept(0, k)
        for copy in x_copies(k):
            copy.wait_recv()
        return total + decode(xrecv[k], xrscale[k])

    def hand_in(s):
        k = class_of(s)
        encode(last(s), zsend.at[k], zsscale.at[k])
        for copy in z_copies(k, (c - k + 3) % 4):
            copy.start()

    def middle(i, carry):
        give(0, class_of(i))
        step(EARLY + 4 + i, carry)
        hand_in(i)
        return carry

    lax.fori_loop(0, 2, middle, 0)
    step(STEPS + 1, 0)
    give(0, class_of(2))
    give(0, class_of(3))
    hand_in(2)
    own[...] = last(3)

    total = own[...]
    for slot in range(3):
        for copy in z_copies((c + 1) % 4, slot):
            copy.wait_recv()
        total = total + decode(zrecv[slot], zrscale[slot])
    own[...] = total
    for p in range(PB):
        turned = own[p * BLOCK : (p + 1) * BLOCK, :].T
        out[0, p, :, 0:BLOCK] = turned[0:BLOCK]
        out[0, p, :, BLOCK:128] = turned[BLOCK:128]

    def sent(u, carry):
        hand(u).wait_send()
        for copy in part_copies(u):
            copy.wait_send()
        return carry

    lax.fori_loop(0, STEPS, sent, 0)
    for copy in weights():
        copy.wait_send()
    for way in range(2):
        for part in range(2):
            halo(way, part).wait_send()
    for n in range(8):
        core_copy(n).wait_send()
    for n in range(4):
        for copy in x_copies(n):
            copy.wait_send()
    for n in range(1, 4):
        for copy in z_copies((c + n) % 4, 0):
            copy.wait_send()


def body(green, broadening, quad_weight, pair_cols):
    vmem, smem = pl.BlockSpec(memory_space=pltpu.VMEM), pl.BlockSpec(memory_space=pltpu.SMEM)
    hbm = pl.BlockSpec(memory_space=pl.ANY)
    dma = pltpu.SemaphoreType.DMA
    return pl.pallas_call(
        kernel,
        out_shape=jax.ShapeDtypeStruct((1, PB, BLOCK, 2 * BLOCK), jnp.float32),
        in_specs=[hbm, hbm, smem, smem],
        out_specs=vmem,
        scratch_shapes=[
            pltpu.VMEM((2, 16, BLOCK, 1024), jnp.bfloat16),
            pltpu.VMEM((2, 48, BLOCK, 256), jnp.bfloat16),
            pltpu.VMEM((2, 48, BLOCK, 256), jnp.bfloat16),
            pltpu.VMEM((8, 1024, 128), jnp.float32),
            pltpu.VMEM((2, 1024, 512), jnp.bfloat16),
            pltpu.VMEM((2, 1024, 512), jnp.bfloat16),
            pltpu.VMEM((2, 512, 512), jnp.bfloat16),
            pltpu.VMEM((2, 256, 512), jnp.bfloat16),
            pltpu.VMEM((16, 128, 1024), jnp.bfloat16),
            pltpu.VMEM((STEPS, BLOCK, 1024), jnp.int16),
            pltpu.VMEM((STEPS, BLOCK, 1024), jnp.int16),
            pltpu.VMEM((STEPS, 8, 128), jnp.float32),
            pltpu.VMEM((STEPS, 8, 128), jnp.float32),
            pltpu.VMEM((8, 1024, 128), jnp.float32),
            pltpu.VMEM((8, 1024, 128), jnp.float32),
            pltpu.VMEM((4, 1024, 128), jnp.int16),
            pltpu.VMEM((4, 1024, 128), jnp.int16),
            pltpu.VMEM((4, 8, 128), jnp.float32),
            pltpu.VMEM((4, 8, 128), jnp.float32),
            pltpu.VMEM((4, 1024, 128), jnp.int16),
            pltpu.VMEM((3, 1024, 128), jnp.int16),
            pltpu.VMEM((4, 8, 128), jnp.float32),
            pltpu.VMEM((3, 8, 128), jnp.float32),
            pltpu.VMEM((1024, 128), jnp.float32),
            dma((6,)), dma((2,)), dma((2,)),
            dma((STEPS,)), dma((STEPS,)), dma((STEPS,)), dma((STEPS,)), dma((STEPS,)), dma((STEPS,)),
            dma((2, 2)), dma((2, 2)),
            dma((8,)), dma((8,)),
            dma((4,)), dma((4,)), dma((4,)), dma((4,)),
            dma((4,)), dma((3,)), dma((4,)), dma((3,)),
        ],
        compiler_params=pltpu.CompilerParams(
            collective_id=0, has_side_effects=True, vmem_limit_bytes=56 * 1024 * 1024
        ),
        cost_estimate=pl.CostEstimate(flops=13 * 10**9, bytes_accessed=7 * 2**20, transcendentals=0),
        name="density",
    )(green.reshape(1, 2, 16, BLOCK, 512), broadening, quad_weight, pair_cols)


def solution(mesh):
    placed = (
        P("energy", None, "row", "col"),
        P("energy", None, None, "col"),
        P("energy"),
        P("row"),
    )
    return jax.shard_map(
        body,
        mesh=mesh,
        in_specs=placed,
        out_specs=P("row", ("energy", "col"), None, None),
        check_vma=False,
    )
```

```python
import functools

import jax
import jax.numpy as jnp
from jax import lax
from jax.experimental import pallas as pl
from jax.experimental.pallas import tpu as pltpu
from jax.sharding import PartitionSpec as P

MESH = pl.DeviceIdType.MESH
NT = (((1,), (1,)), ((), ()))
BLOCK = 64
PB = 16
TOP = 32766.0
STEPS = 16
LEAD = 3
EARLY = 11


def scaled(total, peak):
    peak = jnp.maximum(peak, 1e-30)
    return total * (TOP / peak), peak * (1.0 / TOP)


def coded(values):
    return jnp.round(values).astype(jnp.int32).astype(jnp.int16)


def encode(total, codes, scale):
    values, unit = scaled(total, jnp.max(jnp.abs(total), axis=0, keepdims=True))
    codes[...] = coded(values)
    scale[...] = jnp.broadcast_to(unit, scale.shape)


def decode(codes, scale):
    return codes[...].astype(jnp.int32).astype(jnp.float32) * scale[0:1, :]


def kernel(
    green, gamma, weight, pairs, out,
    held, near_a, near_b, begun, mine, theirs, turn, given, spec, psend, precv, psscale, prscale,
    csend, crecv, csscale, crscale, xsend, xrecv, xsscale, xrscale, zsend, zrecv, zsscale, zrscale, own,
    loc, ws, wr, gs, gr, ps, pr, pss, prs, ys, yr, cs, cr, css, crs, xs, xr, xss, xrs, zs, zr, zss, zrs,
):
    near = (near_a, near_b)
    e, r, c = lax.axis_index("energy"), lax.axis_index("row"), lax.axis_index("col")
    xbit, core = e // 2, e % 2
    pair, cross = c + 1 - 2 * (c % 2), 3 - c
    above, below = (r + 1) % 8, (r + 7) % 8
    core_peer, x_peer = (e + 1 - 2 * core, r, c), (e + 2 - 4 * xbit, r, c)
    pair_peer, cross_peer = (e, r, pair), (e, r, cross)

    def quarter(owner, count=512):
        return pl.ds(pl.multiple_of(owner * 512, 512), count)

    def block_of(u):
        dx, dk, k = 1 - u // 8, 1 - (u // 4) % 2, u % 4
        return ((xbit + dx) % 2) * 8 + ((core + dk) % 2) * 4 + k

    def remote(src, dst, send, recv, peer):
        return pltpu.make_async_remote_copy(
            src_ref=src, dst_ref=dst, send_sem=send, recv_sem=recv, device_id=peer, device_id_type=MESH
        )

    def hand(u):
        b = block_of(u)
        return remote(
            green.at[0, :, b], held.at[:, b, :, pl.ds(512, 512)], gs.at[u], gr.at[u], cross_peer
        )

    def weights():
        return (
            remote(gamma.at[0, :, quarter(3 - pair, 256), :], given, ws.at[0], wr.at[0], cross_peer),
            remote(
                gamma.at[0, :, quarter(3 - pair), pl.ds(256, 256)],
                theirs.at[:, pl.ds(512, 512), pl.ds(256, 256)], ws.at[1], wr.at[1], pair_peer,
            ),
        )

    def part_copies(u):
        return (
            remote(psend.at[u], precv.at[u], ps.at[u], pr.at[u], pair_peer),
            remote(psscale.at[u], prscale.at[u], pss.at[u], prs.at[u], pair_peer),
        )

    def halo(way, part):
        return remote(
            green.at[0, :, :, :, pl.ds(256 * part, 256)], near[part].at[:, pl.ds(32 * way, 16)],
            ys.at[way, part], yr.at[way, part], (e, (above, below)[way], c),
        )

    def core_copies(n):
        return (
            remote(csend.at[n], crecv.at[n], cs.at[n], cr.at[n], core_peer),
            remote(csscale.at[n], crscale.at[n], css.at[n], crs.at[n], core_peer),
        )

    def x_copies(n):
        return (
            remote(xsend.at[n], xrecv.at[n], xs.at[n], xr.at[n], x_peer),
            remote(xsscale.at[n], xrscale.at[n], xss.at[n], xrs.at[n], x_peer),
        )

    def z_copies(k, slot):
        return (
            remote(zsend.at[k], zrecv.at[slot], zs.at[k], zr.at[slot], (e, r, k)),
            remote(zsscale.at[k], zrscale.at[slot], zss.at[k], zrs.at[slot], (e, r, k)),
        )

    locals_ = [
        pltpu.make_async_copy(gamma.at[0, :, quarter(pair), :], turn, loc.at[0]),
        pltpu.make_async_copy(gamma.at[0, :, quarter(c), :], mine.at[:, pl.ds(0, 512), :], loc.at[1]),
        pltpu.make_async_copy(gamma.at[0, :, quarter(cross), :], mine.at[:, pl.ds(512, 512), :], loc.at[2]),
        pltpu.make_async_copy(green.at[0], held.at[:, :, :, pl.ds(0, 512)], loc.at[3]),
        pltpu.make_async_copy(green.at[0, :, :, :, pl.ds(0, 256)], near_a.at[:, pl.ds(16, 16)], loc.at[4]),
        pltpu.make_async_copy(green.at[0, :, :, :, pl.ds(256, 256)], near_b.at[:, pl.ds(16, 16)], loc.at[5]),
    ]
    for copy in locals_:
        copy.start()

    barrier = pltpu.get_barrier_semaphore()
    peers = (core_peer, x_peer, pair_peer, cross_peer, (e, r, (c + 2) % 4), (e, above, c), (e, below, c))
    for peer in peers:
        pl.semaphore_signal(barrier, inc=1, device_id=peer, device_id_type=MESH)
    pl.semaphore_wait(barrier, len(peers))

    for copy in weights():
        copy.start()
    for u in range(LEAD):
        hand(u).start()

    def sends(way):
        return r < 7 if way == 0 else r > 0

    def halo_start(part):
        for way in range(2):
            @pl.when(sends(way))
            def _():
                halo(way, part).start()

    def halo_wait(part):
        for way in range(2):
            @pl.when(sends(1 - way))
            def _():
                halo(way, part).wait_recv()

    halo_start(0)
    for copy in locals_:
        copy.wait()
    theirs[0, 0:512, :] = turn[0].T
    theirs[1, 0:512, :] = -(turn[1].T)
    for copy in weights():
        copy.wait_recv()
    theirs[0, 512:1024, 0:256] = given[0].T
    theirs[1, 512:1024, 0:256] = -(given[1].T)

    def product(b, right):
        left = held[:, b].reshape(2 * BLOCK, 1024)
        with_re = jnp.dot(left, right[0], preferred_element_type=jnp.float32)
        with_im = jnp.dot(left, right[1], preferred_element_type=jnp.float32)
        return jnp.concatenate(
            [with_re[:BLOCK] - with_im[BLOCK:], with_im[:BLOCK] + with_re[BLOCK:]], axis=1
        )

    def forward(u):
        @pl.when(u < STEPS - LEAD)
        def _():
            hand(u + LEAD).start()

        hand(u).wait_recv()
        part = product(block_of(u), theirs)
        peak = jnp.max(jnp.abs(part), axis=0, keepdims=True)
        peak = functools.reduce(jnp.maximum, [peak[:, 128 * i : 128 * (i + 1)] for i in range(8)])
        wide = jnp.concatenate([peak] * 8, axis=1)
        values, unit = scaled(part, wide)
        psend[u] = coded(values)
        psscale[u] = jnp.broadcast_to(unit[:, 0:128], (8, 128))
        for copy in part_copies(u):
            copy.start()

    def spectral(u):
        b = block_of(u)
        part = product(b, mine)
        for copy in part_copies(u):
            copy.wait_recv()
        unit = jnp.concatenate([prscale[u][0:1, :]] * 8, axis=1)
        whole = part + precv[u].astype(jnp.int32).astype(jnp.float32) * unit
        whole = whole.astype(jnp.bfloat16)
        spec[b, 0:BLOCK, :] = whole
        spec[b, BLOCK:128, 0:512] = whole[:, 512:]
        spec[b, BLOCK:128, 512:1024] = -whole[:, :512]

    def terms(dx, dk, k, part):
        block = ((xbit + dx) % 2) * 8 + ((core + dk) % 2) * 4 + k
        at = [jnp.clip(pairs[block * PB + p] - (r - 1) * PB, 0, 47) for p in range(PB)]
        right_re = jnp.concatenate([near[part][0, o] for o in at], axis=0)
        right_im = jnp.concatenate([near[part][1, o] for o in at], axis=0)
        left_re = spec[block, :, 256 * part : 256 * part + 256]
        left_im = spec[block, :, 512 + 256 * part : 768 + 256 * part]
        found = lax.dot_general(right_re, left_re, NT, preferred_element_type=jnp.float32)
        return found + lax.dot_general(right_im, left_im, NT, preferred_element_type=jnp.float32)

    def both(dx, dk, k):
        n = (1 - dk) * 4 + k
        first = begun[n] if dx else terms(dx, dk, k, 0)
        return (first + terms(dx, dk, k, 1)) * weight[0]

    def give(dx, k):
        n = (1 - dx) * 4 + k
        encode(both(dx, 1, k), csend.at[n], csscale.at[n])
        for copy in core_copies(n):
            copy.start()

    def kept(dx, k):
        n = (1 - dx) * 4 + k
        found = both(dx, 0, k)
        for copy in core_copies(n):
            copy.wait_recv()
        return found + decode(crecv[n], crscale[n])

    def class_of(s):
        return jnp.where(s == 3, c, jnp.where(s < c, s, s + 1))

    def step(u, carry):
        @pl.when(u < STEPS)
        def _():
            forward(u)

        @pl.when(u > 1)
        def _():
            spectral(u - 2)

        return carry

    def step_and_begin(u, carry):
        step(u, carry)
        n = u - 3
        begun[n] = terms(1, 1 - n // 4, n % 4, 0)
        return carry

    lax.fori_loop(0, 2, step, 0)
    halo_start(1)
    lax.fori_loop(2, 3, step, 0)
    halo_wait(0)
    lax.fori_loop(3, EARLY, step_and_begin, 0)
    halo_wait(1)
    give(1, class_of(0))

    def early(s, carry):
        step(EARLY + s, carry)
        k = class_of(s)

        @pl.when(s < 3)
        def _():
            give(1, class_of(s + 1))

        encode(kept(1, k), xsend.at[k], xsscale.at[k])
        for copy in x_copies(k):
            copy.start()
        return carry

    lax.fori_loop(0, 4, early, 0)

    def last(s):
        k = class_of(s)
        total = kept(0, k)
        for copy in x_copies(k):
            copy.wait_recv()
        return total + decode(xrecv[k], xrscale[k])

    def hand_in(s):
        k = class_of(s)
        encode(last(s), zsend.at[k], zsscale.at[k])
        for copy in z_copies(k, (c - k + 3) % 4):
            copy.start()

    def middle(i, carry):
        give(0, class_of(i))

        @pl.when(i < 2)
        def _():
            step(EARLY + 4 + i, 0)

        @pl.when(i > 0)
        def _():
            hand_in(i - 1)

        return carry

    lax.fori_loop(0, 3, middle, 0)
    step(STEPS + 1, 0)
    hand_in(2)
    give(0, c)
    own[...] = last(3)

    total = own[...]
    for slot in range(3):
        for copy in z_copies((c + 1) % 4, slot):
            copy.wait_recv()
        total = total + decode(zrecv[slot], zrscale[slot])
    own[...] = total
    for p in range(PB):
        turned = own[p * BLOCK : (p + 1) * BLOCK, :].T
        out[0, p, :, 0:BLOCK] = turned[0:BLOCK]
        out[0, p, :, BLOCK:128] = turned[BLOCK:128]

    def sent(u, carry):
        hand(u).wait_send()
        for copy in part_copies(u):
            copy.wait_send()
        return carry

    lax.fori_loop(0, STEPS, sent, 0)
    for copy in weights():
        copy.wait_send()
    for way in range(2):
        @pl.when(sends(way))
        def _():
            for part in range(2):
                halo(way, part).wait_send()
    for n in range(8):
        for copy in core_copies(n):
            copy.wait_send()
    for n in range(4):
        for copy in x_copies(n):
            copy.wait_send()
    for n in range(1, 4):
        for copy in z_copies((c + n) % 4, 0):
            copy.wait_send()


def body(green, broadening, quad_weight, pair_cols):
    vmem, smem = pl.BlockSpec(memory_space=pltpu.VMEM), pl.BlockSpec(memory_space=pltpu.SMEM)
    hbm = pl.BlockSpec(memory_space=pl.ANY)
    dma = pltpu.SemaphoreType.DMA
    return pl.pallas_call(
        kernel,
        out_shape=jax.ShapeDtypeStruct((1, PB, BLOCK, 2 * BLOCK), jnp.float32),
        in_specs=[hbm, hbm, smem, smem],
        out_specs=vmem,
        scratch_shapes=[
            pltpu.VMEM((2, 16, BLOCK, 1024), jnp.bfloat16),
            pltpu.VMEM((2, 48, BLOCK, 256), jnp.bfloat16),
            pltpu.VMEM((2, 48, BLOCK, 256), jnp.bfloat16),
            pltpu.VMEM((8, 1024, 128), jnp.float32),
            pltpu.VMEM((2, 1024, 512), jnp.bfloat16),
            pltpu.VMEM((2, 1024, 512), jnp.bfloat16),
            pltpu.VMEM((2, 512, 512), jnp.bfloat16),
            pltpu.VMEM((2, 256, 512), jnp.bfloat16),
            pltpu.VMEM((16, 128, 1024), jnp.bfloat16),
            pltpu.VMEM((STEPS, BLOCK, 1024), jnp.int16),
            pltpu.VMEM((STEPS, BLOCK, 1024), jnp.int16),
            pltpu.VMEM((STEPS, 8, 128), jnp.float32),
            pltpu.VMEM((STEPS, 8, 128), jnp.float32),
            pltpu.VMEM((8, 1024, 128), jnp.int16),
            pltpu.VMEM((8, 1024, 128), jnp.int16),
            pltpu.VMEM((8, 8, 128), jnp.float32),
            pltpu.VMEM((8, 8, 128), jnp.float32),
            pltpu.VMEM((4, 1024, 128), jnp.int16),
            pltpu.VMEM((4, 1024, 128), jnp.int16),
            pltpu.VMEM((4, 8, 128), jnp.float32),
            pltpu.VMEM((4, 8, 128), jnp.float32),
            pltpu.VMEM((4, 1024, 128), jnp.int16),
            pltpu.VMEM((3, 1024, 128), jnp.int16),
            pltpu.VMEM((4, 8, 128), jnp.float32),
            pltpu.VMEM((3, 8, 128), jnp.float32),
            pltpu.VMEM((1024, 128), jnp.float32),
            dma((6,)), dma((2,)), dma((2,)),
            dma((STEPS,)), dma((STEPS,)), dma((STEPS,)), dma((STEPS,)), dma((STEPS,)), dma((STEPS,)),
            dma((2, 2)), dma((2, 2)),
            dma((8,)), dma((8,)), dma((8,)), dma((8,)),
            dma((4,)), dma((4,)), dma((4,)), dma((4,)),
            dma((4,)), dma((3,)), dma((4,)), dma((3,)),
        ],
        compiler_params=pltpu.CompilerParams(
            collective_id=0, has_side_effects=True, vmem_limit_bytes=56 * 1024 * 1024
        ),
        cost_estimate=pl.CostEstimate(flops=13 * 10**9, bytes_accessed=7 * 2**20, transcendentals=0),
        name="density",
    )(green.reshape(1, 2, 16, BLOCK, 512), broadening, quad_weight, pair_cols)


def solution(mesh):
    placed = (
        P("energy", None, "row", "col"),
        P("energy", None, None, "col"),
        P("energy"),
        P("row"),
    )
    return jax.shard_map(
        body,
        mesh=mesh,
        in_specs=placed,
        out_specs=P("row", ("energy", "col"), None, None),
        check_vma=False,
    )
```

```python
import functools

import jax
import jax.numpy as jnp
from jax import lax
from jax.experimental import pallas as pl
from jax.experimental.pallas import tpu as pltpu
from jax.sharding import PartitionSpec as P

MESH = pl.DeviceIdType.MESH
NT = (((1,), (1,)), ((), ()))
BLOCK = 64
PB = 16
TOP = 32000.0
STEPS = 16
LEAD = 3
EARLY = 11


def encode(total, codes):
    rows = total.shape[0]
    power = jnp.ceil(jnp.log2(jnp.maximum(jnp.max(jnp.abs(total), axis=0, keepdims=True), 1e-30)))
    codes[0:rows] = jnp.round(total * (TOP * jnp.exp2(-power))).astype(jnp.int32).astype(jnp.int16)
    codes[rows : rows + 16] = jnp.broadcast_to(power, (16, 128)).astype(jnp.int32).astype(jnp.int16)


def decode(codes):
    rows = codes.shape[0] - 16
    power = codes[rows:][0:1].astype(jnp.int32).astype(jnp.float32)
    return codes[0:rows].astype(jnp.int32).astype(jnp.float32) * (jnp.exp2(power) * (1.0 / TOP))


def kernel(
    green, gamma, weight, pairs, out,
    held, near_a, near_b, begun, mine, theirs, turn, given, spec, psend, precv,
    csend, crecv, xsend, xrecv, zsend, zrecv, own,
    loc, ws, wr, gs, gr, ps, pr, ys, yr, cs, cr, xs, xr, zs, zr,
):
    near = (near_a, near_b)
    e, r, c = lax.axis_index("energy"), lax.axis_index("row"), lax.axis_index("col")
    xbit, core = e // 2, e % 2
    pair, cross = c + 1 - 2 * (c % 2), 3 - c
    above, below = (r + 1) % 8, (r + 7) % 8
    core_peer, x_peer = (e + 1 - 2 * core, r, c), (e + 2 - 4 * xbit, r, c)
    pair_peer, cross_peer = (e, r, pair), (e, r, cross)

    def quarter(owner, count=512):
        return pl.ds(pl.multiple_of(owner * 512, 512), count)

    def block_of(u):
        dx, dk, k = 1 - u // 8, 1 - (u // 4) % 2, u % 4
        return ((xbit + dx) % 2) * 8 + ((core + dk) % 2) * 4 + k

    def remote(src, dst, send, recv, peer):
        return pltpu.make_async_remote_copy(
            src_ref=src, dst_ref=dst, send_sem=send, recv_sem=recv, device_id=peer, device_id_type=MESH
        )

    def hand(u):
        b = block_of(u)
        return remote(
            green.at[0, :, b], held.at[:, b, :, pl.ds(512, 512)], gs.at[u], gr.at[u], cross_peer
        )

    def weights():
        return (
            remote(gamma.at[0, :, quarter(3 - pair, 256), :], given, ws.at[0], wr.at[0], cross_peer),
            remote(
                gamma.at[0, :, quarter(3 - pair), pl.ds(256, 256)],
                theirs.at[:, pl.ds(512, 512), pl.ds(256, 256)], ws.at[1], wr.at[1], pair_peer,
            ),
        )

    def part_copies(u):
        return (
            remote(psend.at[u], precv.at[u], ps.at[u], pr.at[u], pair_peer),
        )

    def halo(way, part):
        return remote(
            green.at[0, :, :, :, pl.ds(256 * part, 256)], near[part].at[:, pl.ds(32 * way, 16)],
            ys.at[way, part], yr.at[way, part], (e, (above, below)[way], c),
        )

    def core_copies(n):
        return (
            remote(csend.at[n], crecv.at[n], cs.at[n], cr.at[n], core_peer),
        )

    def x_copies(n):
        return (
            remote(xsend.at[n], xrecv.at[n], xs.at[n], xr.at[n], x_peer),
        )

    def z_copies(k, slot):
        return (
            remote(zsend.at[k], zrecv.at[slot], zs.at[k], zr.at[slot], (e, r, k)),
        )

    locals_ = [
        pltpu.make_async_copy(gamma.at[0, :, quarter(pair), :], turn, loc.at[0]),
        pltpu.make_async_copy(gamma.at[0, :, quarter(c), :], mine.at[:, pl.ds(0, 512), :], loc.at[1]),
        pltpu.make_async_copy(gamma.at[0, :, quarter(cross), :], mine.at[:, pl.ds(512, 512), :], loc.at[2]),
        pltpu.make_async_copy(green.at[0], held.at[:, :, :, pl.ds(0, 512)], loc.at[3]),
        pltpu.make_async_copy(green.at[0, :, :, :, pl.ds(0, 256)], near_a.at[:, pl.ds(16, 16)], loc.at[4]),
        pltpu.make_async_copy(green.at[0, :, :, :, pl.ds(256, 256)], near_b.at[:, pl.ds(16, 16)], loc.at[5]),
    ]
    for copy in locals_:
        copy.start()

    barrier = pltpu.get_barrier_semaphore()
    peers = (core_peer, x_peer, pair_peer, cross_peer, (e, r, (c + 2) % 4), (e, above, c), (e, below, c))
    for peer in peers:
        pl.semaphore_signal(barrier, inc=1, device_id=peer, device_id_type=MESH)
    pl.semaphore_wait(barrier, len(peers))

    for copy in weights():
        copy.start()
    for u in range(LEAD):
        hand(u).start()

    def sends(way):
        return r < 7 if way == 0 else r > 0

    def halo_start(part):
        for way in range(2):
            @pl.when(sends(way))
            def _():
                halo(way, part).start()

    def halo_wait(part):
        for way in range(2):
            @pl.when(sends(1 - way))
            def _():
                halo(way, part).wait_recv()

    halo_start(0)
    for copy in locals_:
        copy.wait()
    theirs[0, 0:512, :] = turn[0].T
    theirs[1, 0:512, :] = -(turn[1].T)
    for copy in weights():
        copy.wait_recv()
    theirs[0, 512:1024, 0:256] = given[0].T
    theirs[1, 512:1024, 0:256] = -(given[1].T)

    def product(b, right):
        left = held[:, b].reshape(2 * BLOCK, 1024)
        with_re = jnp.dot(left, right[0], preferred_element_type=jnp.float32)
        with_im = jnp.dot(left, right[1], preferred_element_type=jnp.float32)
        return jnp.concatenate(
            [with_re[:BLOCK] - with_im[BLOCK:], with_im[:BLOCK] + with_re[BLOCK:]], axis=1
        )

    def forward(u):
        @pl.when(u < STEPS - LEAD)
        def _():
            hand(u + LEAD).start()

        hand(u).wait_recv()
        part = product(block_of(u), theirs)
        encode(jnp.concatenate([part[:, 128 * i : 128 * (i + 1)] for i in range(8)], axis=0), psend.at[u])
        for copy in part_copies(u):
            copy.start()

    def spectral(u):
        b = block_of(u)
        part = product(b, mine)
        for copy in part_copies(u):
            copy.wait_recv()
        other = decode(precv.at[u])
        whole = part + jnp.concatenate([other[BLOCK * i : BLOCK * (i + 1)] for i in range(8)], axis=1)
        whole = whole.astype(jnp.bfloat16)
        spec[b, 0:BLOCK, :] = whole
        spec[b, BLOCK:128, 0:512] = whole[:, 512:]
        spec[b, BLOCK:128, 512:1024] = -whole[:, :512]

    def terms(dx, dk, k, part):
        block = ((xbit + dx) % 2) * 8 + ((core + dk) % 2) * 4 + k
        at = [jnp.clip(pairs[block * PB + p] - (r - 1) * PB, 0, 47) for p in range(PB)]
        right_re = jnp.concatenate([near[part][0, o] for o in at], axis=0)
        right_im = jnp.concatenate([near[part][1, o] for o in at], axis=0)
        left_re = spec[block, :, 256 * part : 256 * part + 256]
        left_im = spec[block, :, 512 + 256 * part : 768 + 256 * part]
        found = lax.dot_general(right_re, left_re, NT, preferred_element_type=jnp.float32)
        return found + lax.dot_general(right_im, left_im, NT, preferred_element_type=jnp.float32)

    def both(dx, dk, k):
        n = (1 - dk) * 4 + k
        first = begun[n] if dx else terms(dx, dk, k, 0)
        return (first + terms(dx, dk, k, 1)) * weight[0]

    def give(dx, k):
        n = (1 - dx) * 4 + k
        encode(both(dx, 1, k), csend.at[n])
        for copy in core_copies(n):
            copy.start()

    def kept(dx, k):
        n = (1 - dx) * 4 + k
        found = both(dx, 0, k)
        for copy in core_copies(n):
            copy.wait_recv()
        return found + decode(crecv.at[n])

    def class_of(s):
        return jnp.where(s == 3, c, jnp.where(s < c, s, s + 1))

    def step(u, carry):
        @pl.when(u < STEPS)
        def _():
            forward(u)

        @pl.when(u > 1)
        def _():
            spectral(u - 2)

        return carry

    def step_and_begin(u, carry):
        step(u, carry)
        n = u - 3
        begun[n] = terms(1, 1 - n // 4, n % 4, 0)
        return carry

    lax.fori_loop(0, 2, step, 0)
    halo_start(1)
    lax.fori_loop(2, 3, step, 0)
    halo_wait(0)
    lax.fori_loop(3, EARLY, step_and_begin, 0)
    halo_wait(1)
    give(1, class_of(0))

    def early(s, carry):
        step(EARLY + s, carry)
        k = class_of(s)

        @pl.when(s < 3)
        def _():
            give(1, class_of(s + 1))

        encode(kept(1, k), xsend.at[k])
        for copy in x_copies(k):
            copy.start()
        return carry

    lax.fori_loop(0, 4, early, 0)

    def last(s):
        k = class_of(s)
        total = kept(0, k)
        for copy in x_copies(k):
            copy.wait_recv()
        return total + decode(xrecv.at[k])

    def hand_in(s):
        k = class_of(s)
        encode(last(s), zsend.at[k])
        for copy in z_copies(k, (c - k + 3) % 4):
            copy.start()

    def middle(i, carry):
        give(0, class_of(i))

        @pl.when(i < 2)
        def _():
            step(EARLY + 4 + i, 0)

        @pl.when(i > 0)
        def _():
            hand_in(i - 1)

        return carry

    lax.fori_loop(0, 3, middle, 0)
    step(STEPS + 1, 0)
    hand_in(2)
    give(0, c)
    own[...] = last(3)

    total = own[...]
    for slot in range(3):
        for copy in z_copies((c + 1) % 4, slot):
            copy.wait_recv()
        total = total + decode(zrecv.at[slot])
    own[...] = total
    for p in range(PB):
        turned = own[p * BLOCK : (p + 1) * BLOCK, :].T
        out[0, p, :, 0:BLOCK] = turned[0:BLOCK]
        out[0, p, :, BLOCK:128] = turned[BLOCK:128]

    def sent(u, carry):
        hand(u).wait_send()
        for copy in part_copies(u):
            copy.wait_send()
        return carry

    lax.fori_loop(0, STEPS, sent, 0)
    for copy in weights():
        copy.wait_send()
    for way in range(2):
        @pl.when(sends(way))
        def _():
            for part in range(2):
                halo(way, part).wait_send()
    for n in range(8):
        for copy in core_copies(n):
            copy.wait_send()
    for n in range(4):
        for copy in x_copies(n):
            copy.wait_send()
    for n in range(1, 4):
        for copy in z_copies((c + n) % 4, 0):
            copy.wait_send()


def body(green, broadening, quad_weight, pair_cols):
    vmem, smem = pl.BlockSpec(memory_space=pltpu.VMEM), pl.BlockSpec(memory_space=pltpu.SMEM)
    hbm = pl.BlockSpec(memory_space=pl.ANY)
    dma = pltpu.SemaphoreType.DMA
    return pl.pallas_call(
        kernel,
        out_shape=jax.ShapeDtypeStruct((1, PB, BLOCK, 2 * BLOCK), jnp.float32),
        in_specs=[hbm, hbm, smem, smem],
        out_specs=vmem,
        scratch_shapes=[
            pltpu.VMEM((2, 16, BLOCK, 1024), jnp.bfloat16),
            pltpu.VMEM((2, 48, BLOCK, 256), jnp.bfloat16),
            pltpu.VMEM((2, 48, BLOCK, 256), jnp.bfloat16),
            pltpu.VMEM((8, 1024, 128), jnp.float32),
            pltpu.VMEM((2, 1024, 512), jnp.bfloat16),
            pltpu.VMEM((2, 1024, 512), jnp.bfloat16),
            pltpu.VMEM((2, 512, 512), jnp.bfloat16),
            pltpu.VMEM((2, 256, 512), jnp.bfloat16),
            pltpu.VMEM((16, 128, 1024), jnp.bfloat16),
            pltpu.VMEM((STEPS, 528, 128), jnp.int16),
            pltpu.VMEM((STEPS, 528, 128), jnp.int16),
            pltpu.VMEM((8, 1040, 128), jnp.int16),
            pltpu.VMEM((8, 1040, 128), jnp.int16),
            pltpu.VMEM((4, 1040, 128), jnp.int16),
            pltpu.VMEM((4, 1040, 128), jnp.int16),
            pltpu.VMEM((4, 1040, 128), jnp.int16),
            pltpu.VMEM((3, 1040, 128), jnp.int16),
            pltpu.VMEM((1024, 128), jnp.float32),
            dma((6,)), dma((2,)), dma((2,)),
            dma((STEPS,)), dma((STEPS,)), dma((STEPS,)), dma((STEPS,)),
            dma((2, 2)), dma((2, 2)),
            dma((8,)), dma((8,)),
            dma((4,)), dma((4,)),
            dma((4,)), dma((3,)),
        ],
        compiler_params=pltpu.CompilerParams(
            collective_id=0, has_side_effects=True, vmem_limit_bytes=56 * 1024 * 1024
        ),
        cost_estimate=pl.CostEstimate(flops=13 * 10**9, bytes_accessed=7 * 2**20, transcendentals=0),
        name="density",
    )(green.reshape(1, 2, 16, BLOCK, 512), broadening, quad_weight, pair_cols)


def solution(mesh):
    placed = (
        P("energy", None, "row", "col"),
        P("energy", None, None, "col"),
        P("energy"),
        P("row"),
    )
    return jax.shard_map(
        body,
        mesh=mesh,
        in_specs=placed,
        out_specs=P("row", ("energy", "col"), None, None),
        check_vma=False,
    )
```
